32 devices in a mesh: tile: 8 (over z, y), head: 4 (over x, core).
Axes of the slice: x: 2, y: 2, z: 4, core: 2. Of those that a mesh axis runs over, the one named last changes fastest.
Arguments:
- tokens: bfloat16 [3072, 3072], P('tile'), may hold values from -200 to 200
- mod_shift: float32 [3072], replicated, may hold values from -3 to 3
- mod_scale: float32 [3072], replicated, may hold values from -2.5 to 2.5
- mod_gate: float32 [3072], replicated, may hold values from -4 to 4
- qkv_weight: bfloat16 [3072, 1536], P(None, 'head'), may hold values from -1 to 1
- out_weight: bfloat16 [512, 3072], P('head'), may hold values from -0.25 to 0.25
- teacher: bfloat16 [3072, 3072], P('tile'), may hold values from -6 to 6
- slot_tiles: int32 [8], replicated, may hold values from 0 to 7, each once
Outputs:
- qkv_grad: float32 [3072, 1536], P('tile', 'head')
- out_grad: float32 [512, 3072], P('head', 'tile')
The draws below stay inside these ranges and needn't reach their ends.
Inputs may be any that keep to these rules, and one draw needn't show every extreme that they name: Slot s, rows s * 384 to (s + 1) * 384 - 1 of tokens and teacher, holds tile slot_tiles[s]; every tile once.
All inputs are finite; a program needn't handle non-finite values.
Results may differ from the reference program's by a relative error of at most 0.00049.
Values may be sent and summed in bfloat16 or wider, within the bound.
No kernel may reach another device: no remote copies, remote signals or barrier semaphores. Data moves between devices by JAX's collectives and lax.ppermute only.
A program may use at most 128 MiB of HBM per device.

```python
import math
import jax
import jax.numpy as jnp
from jax import lax

D = 3072
HD = 128
TOK_TILE = 384
TH = 4
HEADS = 4
TILES = 8
TW = 2
TOKENS = 3072


def draw_tokens(key, part):
    base_key, col_key, row_key = jax.random.split(key, 3)
    col_scale = jnp.exp(jax.random.uniform(col_key, (1, D), jnp.float32, 0.0, math.log(10.0)))
    row_scale = jnp.exp(jax.random.uniform(row_key, (TOKENS, 1), jnp.float32, math.log(0.5), math.log(5.0)))
    base_values = jax.random.normal(base_key, (TOKENS, D), jnp.float32)
    return (jnp.clip(base_values, -4.0, 4.0) * col_scale * row_scale).astype(jnp.bfloat16)


def draw_qkv_weight(key, part):
    query_key, noise_key, value_key = jax.random.split(jax.random.fold_in(key, 7), 3)
    fan_scale = 1.0 / math.sqrt(D)
    query_cols = jnp.clip(jax.random.normal(query_key, (D, HEADS, 1, HD), jnp.float32), -6.0, 6.0)
    noise_cols = jnp.clip(jax.random.normal(noise_key, (D, HEADS, 1, HD), jnp.float32), -4.0, 4.0)
    value_cols = jnp.clip(jax.random.normal(value_key, (D, HEADS, 1, HD), jnp.float32), -6.0, 6.0)
    key_cols = query_cols + 0.25 * noise_cols
    joined = jnp.concatenate([query_cols, key_cols, value_cols], 2) * fan_scale
    return joined.reshape(D, HEADS * 3 * HD).astype(jnp.bfloat16)


def levels(stream_key, shape, cuts, smallest, top_value):
    loudness, own = 1.0, jax.random.fold_in(stream_key, 6)
    for axis_at, parts in cuts:
        heights = jnp.exp(jax.random.uniform(jax.random.fold_in(own, axis_at), (parts,), jnp.float32, smallest / len(cuts), top_value / len(cuts)))
        loudness = loudness * jnp.repeat(heights, shape[axis_at] // parts).reshape([-1 if axis == axis_at else 1 for axis in range(len(shape))])
    return loudness


def bell_draw(stream_key, dims, scale, limit, cuts=(), kind=jnp.bfloat16):
    gain = levels(stream_key, dims, cuts, -0.22, 0.18) if cuts else 1.0
    drawn = jax.random.normal(stream_key, dims, jnp.float32) * scale * gain
    return jnp.minimum(jnp.maximum(drawn, -limit), limit).astype(kind)


def setup_inputs(seed: int = 0) -> dict:
    seeds = jax.random.split(jax.random.key(seed), 9)
    return {
        "tokens": draw_tokens(jax.random.fold_in(seeds[8], 71), 0),
        "mod_shift": bell_draw(seeds[1], (D,), 0.5, 3.0, (), jnp.float32),
        "mod_scale": bell_draw(seeds[2], (D,), 0.5, 2.5, (), jnp.float32),
        "mod_gate": bell_draw(seeds[3], (D,), 1.0, 4.0, (), jnp.float32),
        "qkv_weight": draw_qkv_weight(jax.random.fold_in(seeds[8], 71), 0),
        "out_weight": bell_draw(seeds[5], (HEADS * HD, D), (HEADS * HD) ** -0.5, 0.25, ((0, 4),)),
        "teacher": bell_draw(seeds[6], (TOKENS, D), 1.0, 6.0, ((0, 8),)),
        "slot_tiles": jax.random.permutation(seeds[7], TILES).astype(jnp.int32),
    }


EPS_NORM = 1e-05
EPS_ROOT = 1e-06
LOSS_WEIGHT = 32.0

def root_norm(values):
    factor = lax.rsqrt(lax.optimization_barrier(jnp.mean(values * values, -1, keepdims=True)) + EPS_ROOT)
    return (values * factor, factor)

def root_norm_back(grad_unit, unit_value, factor):
    return factor * (grad_unit - unit_value * lax.optimization_barrier(jnp.mean(grad_unit * unit_value, -1, keepdims=True)))

def near_tiles(first_tiles, second_tiles, width_tiles):

    def coords(ids):
        return (ids // (TH * width_tiles), ids // width_tiles % TH, ids % width_tiles)
    ta, ha, wa = coords(first_tiles[:, None])
    tb, hb, wb = coords(second_tiles[None, :])
    close = (jnp.abs(ta - tb) <= 1) & (jnp.abs(ha - hb) <= 1) & (jnp.abs(wa - wb) <= 1)
    return close.astype(jnp.float32)

def reference(tokens, mod_shift, mod_scale, mod_gate, qkv_weight, out_weight, teacher, slot_tiles):
    att_scale = 1.0 / math.sqrt(HD)
    values_in = tokens.astype(jnp.float32)
    center = values_in - lax.optimization_barrier(jnp.mean(values_in, -1, keepdims=True))
    spread = lax.optimization_barrier(jnp.mean(center * center, -1, keepdims=True))
    normed = (center * lax.rsqrt(spread + EPS_NORM) * (1.0 + mod_scale) + mod_shift).astype(jnp.bfloat16)
    projected = jnp.dot(normed, qkv_weight, preferred_element_type=jnp.float32).reshape(TOKENS, HEADS, 3, HD)
    query_unit, query_factor = root_norm(projected[:, :, 0])
    key_unit, key_factor = root_norm(projected[:, :, 1])
    query_b = query_unit.astype(jnp.bfloat16)
    key_b = key_unit.astype(jnp.bfloat16)
    value_b = projected[:, :, 2].astype(jnp.bfloat16)
    tile_mask = near_tiles(slot_tiles, slot_tiles, TW)
    key_full = key_b.astype(jnp.float32)
    value_full = value_b.astype(jnp.float32)

    def tile_weights(tile_index):
        query_tile = lax.dynamic_slice_in_dim(query_b, tile_index * TOK_TILE, TOK_TILE, 0).astype(jnp.float32)
        scores = jnp.einsum('qhd,khd->hqk', query_tile, key_full) * att_scale
        key_mask = jnp.repeat(tile_mask[tile_index], TOK_TILE)
        exp_scores = jnp.exp(scores) * key_mask[None, None, :]
        totals = lax.optimization_barrier(jnp.sum(exp_scores, -1))
        return (query_tile, exp_scores / totals[:, :, None])

    def forward_tile(tile_index):
        query_tile, att_probs = tile_weights(tile_index)
        probs_b = lax.optimization_barrier(att_probs.astype(jnp.bfloat16)).astype(jnp.float32)
        return jnp.einsum('hqk,khd->qhd', probs_b, value_full).astype(jnp.bfloat16)
    tile_ids = jnp.arange(TILES, dtype=jnp.int32)
    attended = lax.map(forward_tile, tile_ids).reshape(TOKENS, HEADS, HD)
    flat_att = attended.reshape(TOKENS, HEADS * HD)
    branch = jnp.dot(flat_att, out_weight, preferred_element_type=jnp.float32)
    residual = LOSS_WEIGHT * (mod_gate * branch - teacher.astype(jnp.float32))
    grad_branch = (mod_gate * residual).astype(jnp.bfloat16)
    out_grad = jnp.dot(flat_att.T, grad_branch, preferred_element_type=jnp.float32)
    grad_att = jnp.dot(grad_branch, out_weight.T, preferred_element_type=jnp.float32)
    grad_att = grad_att.reshape(TOKENS, HEADS, HD).astype(jnp.bfloat16)
    row_delta = lax.optimization_barrier(jnp.sum(grad_att.astype(jnp.float32) * attended.astype(jnp.float32), -1))

    def backward_tile(running, tile_index):
        query_tile, att_probs = tile_weights(tile_index)
        grad_tile = lax.dynamic_slice_in_dim(grad_att, tile_index * TOK_TILE, TOK_TILE, 0).astype(jnp.float32)
        delta_tile = lax.dynamic_slice_in_dim(row_delta, tile_index * TOK_TILE, TOK_TILE, 0)
        grad_probs = jnp.einsum('qhd,khd->hqk', grad_tile, value_full)
        grad_scores = att_probs * (grad_probs - delta_tile.T[:, :, None])
        grad_scores = lax.optimization_barrier(grad_scores.astype(jnp.bfloat16)).astype(jnp.float32)
        probs_b = lax.optimization_barrier(att_probs.astype(jnp.bfloat16)).astype(jnp.float32)
        grad_query_tile = jnp.einsum('hqk,khd->qhd', grad_scores, key_full) * att_scale
        key_sum = running[0] + jnp.einsum('hqk,qhd->khd', grad_scores, query_tile) * att_scale
        value_sum = running[1] + jnp.einsum('hqk,qhd->khd', probs_b, grad_tile)
        return ((key_sum, value_sum), grad_query_tile)
    zero_keys = jnp.zeros((TOKENS, HEADS, HD), jnp.float32)
    (grad_key_unit, grad_value), grad_query_unit = lax.scan(backward_tile, (zero_keys, zero_keys), tile_ids)
    grad_query_unit = grad_query_unit.reshape(TOKENS, HEADS, HD)
    grad_query = root_norm_back(grad_query_unit, query_unit, query_factor)
    grad_key = root_norm_back(grad_key_unit, key_unit, key_factor)
    grad_qkv = jnp.stack([grad_query, grad_key, grad_value], 2).astype(jnp.bfloat16).reshape(TOKENS, HEADS * 3 * HD)
    qkv_grad = jnp.dot(normed.T, grad_qkv, preferred_element_type=jnp.float32)
    return (qkv_grad, out_grad)
```

```python
import functools
import math

import jax
import jax.numpy as jnp
import numpy as np
from jax import lax
from jax.experimental import pallas as pl
from jax.experimental.pallas import tpu as pltpu
from jax.sharding import PartitionSpec as P

HD = 128
TOK_TILE = 384
LANE_ROWS = TOK_TILE // HD
TT = 1
TH = 4


EPS_NORM = 1e-05
EPS_ROOT = 1e-06
LOSS_WEIGHT = 32.0
EXP_SCALE = math.log2(math.e) / math.sqrt(HD)
ATT_SCALE = 1.0 / math.sqrt(HD)
STAT_ROWS = 32
VMEM_BYTES = 56 * 1024 * 1024

NN = (((1,), (0,)), ((), ()))
NT = (((1,), (1,)), ((), ()))
TN = (((0,), (0,)), ((), ()))


def mm(a, b, dims):
    return lax.dot_general(a, b, dims, preferred_element_type=jnp.float32)


def ring_order(count):
    return [*range(0, count, 2), *range(count - 1 - (count % 2), 0, -2)]


def rel_offsets(count):
    offsets = [0]
    for step in range(1, count // 2 + 1):
        offsets.append(-step)
        if len(offsets) < count:
            offsets.append(step)
    return offsets[:count]


def ring_tables(count):
    order = ring_order(count)
    pos = [order.index(slot) for slot in range(count)]
    rels = rel_offsets(count)
    source = [[order[(pos[s] + rel) % count] for rel in rels] for s in range(count)]
    target = [[order[(pos[s] - rel) % count] for rel in rels] for s in range(count)]
    return np.array(source, np.int32), np.array(target, np.int32)


def shift_perm(count, offset):
    order = ring_order(count)
    return [(order[p], order[(p + offset) % count]) for p in range(count)]


def ring_gather(block, count):
    up, down = [block], [block]
    for _ in range(count // 2):
        up.append(lax.ppermute(up[-1], "tile", shift_perm(count, 1)))
    for _ in range((count - 1) // 2):
        down.append(lax.ppermute(down[-1], "tile", shift_perm(count, -1)))
    out = []
    for rel in rel_offsets(count):
        out.append(up[-rel] if rel <= 0 else down[rel])
    return out


def xor_perm(count, mask):
    return [(h, h ^ mask) for h in range(count)]


def head_gather_doubling(block, count):
    blocks = [block]
    mask = count // 2
    masks = [0]
    while mask:
        moved = [lax.ppermute(b, "head", xor_perm(count, mask)) for b in blocks]
        blocks = blocks + moved
        masks = masks + [m ^ mask for m in masks]
        mask //= 2
    return [blocks[masks.index(m)] for m in range(count)]


def head_gather_direct(block, count):
    return [block] + [lax.ppermute(block, "head", xor_perm(count, m)) for m in range(1, count)]


def near_tiles(first_tiles, second_tiles, width_tiles):

    def coords(ids):
        return (ids // (TH * width_tiles), ids // width_tiles % TH, ids % width_tiles)

    ta, ha, wa = coords(first_tiles[:, None])
    tb, hb, wb = coords(second_tiles[None, :])
    close = (jnp.abs(ta - tb) <= 1) & (jnp.abs(ha - hb) <= 1) & (jnp.abs(wa - wb) <= 1)
    return close.astype(jnp.int32)


def split3(row):
    hi = row.astype(jnp.bfloat16).astype(jnp.float32)
    rest = row - hi
    mid = rest.astype(jnp.bfloat16).astype(jnp.float32)
    return [hi, mid, rest - mid]


def pack_rows(rows):
    pieces = [part for row in rows for part in split3(row)]
    pieces.append(jnp.zeros((STAT_ROWS - len(pieces), HD), jnp.float32))
    return jnp.concatenate(pieces, 0).astype(jnp.bfloat16)


def unpack_rows(packed, index):
    wide = packed.astype(jnp.float32)
    rows = []
    for chunk in range(LANE_ROWS):
        at = (index * LANE_ROWS + chunk) * 3
        rows.append(wide[at : at + 1] + wide[at + 1 : at + 2] + wide[at + 2 : at + 3])
    return jnp.concatenate(rows, 1)


def lane_chunks(row):
    return [row[:, c * HD : (c + 1) * HD] for c in range(LANE_ROWS)]


def project_kernel(tok_ref, shift_ref, scale_ref, w_ref, normed_ref, kv_ref, q_ref):
    query_rows, key_rows = [], []
    for chunk in range(LANE_ROWS):
        rows = pl.ds(chunk * HD, HD)
        values_in = tok_ref[rows, :].astype(jnp.float32)
        center = values_in - jnp.mean(values_in, -1, keepdims=True)
        spread = jnp.mean(center * center, -1, keepdims=True)
        normed = (
            center * lax.rsqrt(spread + EPS_NORM) * (1.0 + scale_ref[...]) + shift_ref[...]
        ).astype(jnp.bfloat16)
        normed_ref[rows, :] = normed
        projected = mm(normed, w_ref[...], NN)
        query, key, value = (projected[:, c * HD : (c + 1) * HD] for c in range(3))
        rq = lax.rsqrt(jnp.mean(query * query, -1, keepdims=True) + EPS_ROOT)
        rk = lax.rsqrt(jnp.mean(key * key, -1, keepdims=True) + EPS_ROOT)
        query, key = query * rq, key * rk
        query_b, key_b = query.astype(jnp.bfloat16), key.astype(jnp.bfloat16)
        q_ref[rows, :] = query_b
        q_ref[pl.ds(TOK_TILE + chunk * HD, HD), :] = (
            query - query_b.astype(jnp.float32)
        ).astype(jnp.bfloat16)
        q_ref[pl.ds(2 * TOK_TILE + chunk * HD, HD), :] = (
            key - key_b.astype(jnp.float32)
        ).astype(jnp.bfloat16)
        kv_ref[rows, :] = key_b
        kv_ref[pl.ds(TOK_TILE + chunk * HD, HD), :] = value.astype(jnp.bfloat16)
        query_rows.append(jnp.broadcast_to(rq, (HD, HD)).T[0:1])
        key_rows.append(jnp.broadcast_to(rk, (HD, HD)).T[0:1])
    q_ref[pl.ds(3 * TOK_TILE, STAT_ROWS), :] = pack_rows(query_rows + key_rows)


def attend_kernel(count, allowed_ref, q_ref, *refs):
    kv_refs = refs[:count]
    att_ref, inv_ref, expo, totals, acc = refs[count:]
    query = q_ref[pl.ds(0, TOK_TILE), :]
    totals[...] = jnp.zeros_like(totals)
    acc[...] = jnp.zeros_like(acc)
    for r in range(count):

        @pl.when(allowed_ref[0, r] != 0)
        def _():
            scores = mm(kv_refs[r][pl.ds(0, TOK_TILE), :], query, NT)
            part = jnp.exp2(scores * EXP_SCALE)
            expo[r] = part
            totals[...] += jnp.sum(part, 0, keepdims=True)

    inverse = 1.0 / totals[...]
    inv_ref[...] = inverse
    for r in range(count):

        @pl.when(allowed_ref[0, r] != 0)
        def _():
            probs = (expo[r] * inverse).astype(jnp.bfloat16)
            acc[...] += mm(kv_refs[r][pl.ds(TOK_TILE, TOK_TILE), :], probs, TN)

    att_ref[...] = acc[...].T.astype(jnp.bfloat16)


def branch_kernel(heads, inv_ref, gate_ref, teacher_ref, *refs):
    att_refs = refs[:heads]
    w_refs = refs[heads : 2 * heads]
    ga_ref, out_ref, acc = refs[2 * heads :]
    step = pl.program_id(0)

    @pl.when(step == 0)
    def _():
        acc[...] = jnp.zeros_like(acc)

    branch = mm(att_refs[0][...], w_refs[0][...], NN)
    for h in range(1, heads):
        branch += mm(att_refs[h][...], w_refs[h][...], NN)
    gate = gate_ref[...]
    residual = LOSS_WEIGHT * (gate * branch - teacher_ref[...].astype(jnp.float32))
    grad = (gate * residual).astype(jnp.bfloat16)
    out_ref[...] = mm(att_refs[0][...], grad, TN)
    acc[...] += mm(grad, w_refs[0][...], NT)

    @pl.when(step == pl.num_programs(0) - 1)
    def _():
        grad_att = acc[...].astype(jnp.bfloat16)
        ga_ref[pl.ds(0, TOK_TILE), :] = grad_att
        product = grad_att.astype(jnp.float32) * att_refs[0][...].astype(jnp.float32)
        delta = jnp.sum(product.T, 0, keepdims=True)
        ga_ref[pl.ds(TOK_TILE, STAT_ROWS), :] = pack_rows(
            lane_chunks(inv_ref[...]) + lane_chunks(delta)
        )


def backward_kernel(count, allowed_ref, *refs):
    kv_in, q_in, ga_in = refs[:count], refs[count : 2 * count], refs[2 * count : 3 * count]
    nb_in = refs[3 * count]
    out_ref = refs[3 * count + 1]
    kv, qq, ga, nb, dq, dk, dv, grads, sems = refs[3 * count + 2 :]
    copies = []
    for r in range(count):
        copies.append(pltpu.make_async_copy(kv_in[r], kv.at[r], sems.at[3 * r]))
        copies.append(pltpu.make_async_copy(q_in[r], qq.at[r], sems.at[3 * r + 1]))
        copies.append(pltpu.make_async_copy(ga_in[r], ga.at[r], sems.at[3 * r + 2]))
    copies.append(pltpu.make_async_copy(nb_in, nb, sems.at[3 * count]))
    for copy in copies:
        copy.start()
    dk[...] = jnp.zeros_like(dk)
    dv[...] = jnp.zeros_like(dv)
    for copy in copies:
        copy.wait()
    first = pl.ds(0, TOK_TILE)
    second = pl.ds(TOK_TILE, TOK_TILE)
    stats = pl.ds(TOK_TILE, STAT_ROWS)

    def per_query(i, carry):
        query = qq[i, first, :]
        grad = ga[i, first, :]
        packed = ga[i, stats, :]
        inverse, delta = unpack_rows(packed, 0), unpack_rows(packed, 1)
        dq[...] = jnp.zeros_like(dq)

        def per_key(j, carry):
            @pl.when(allowed_ref[i, j] != 0)
            def _():
                key = kv[j, first, :]
                value = kv[j, second, :]
                scores = mm(key, query, NT)
                probs = jnp.exp2(scores * EXP_SCALE) * inverse
                grad_probs = mm(value, grad, NT)
                grad_scores = (probs * (grad_probs - delta)).astype(jnp.bfloat16)
                dv[j] += mm(probs.astype(jnp.bfloat16), grad, NN)
                dk[j] += mm(grad_scores, query, NN)
                dq[...] += mm(key, grad_scores, TN)

            return carry

        lax.fori_loop(0, count, per_key, 0)
        query_unit = query.astype(jnp.float32) + qq[i, second, :].astype(jnp.float32)
        factor = unpack_rows(qq[i, pl.ds(3 * TOK_TILE, STAT_ROWS), :], 0)
        grads[i, :, pl.ds(0, HD)] = root_back(dq[...].T * ATT_SCALE, query_unit, factor)
        return carry

    lax.fori_loop(0, count, per_query, 0)

    def finish(j, carry):
        key_unit = kv[j, first, :].astype(jnp.float32) + qq[
            j, pl.ds(2 * TOK_TILE, TOK_TILE), :
        ].astype(jnp.float32)
        factor = unpack_rows(qq[j, pl.ds(3 * TOK_TILE, STAT_ROWS), :], 1)
        grads[j, :, pl.ds(HD, HD)] = root_back(dk[j] * ATT_SCALE, key_unit, factor)
        grads[j, :, pl.ds(2 * HD, HD)] = dv[j].astype(jnp.bfloat16)
        return carry

    lax.fori_loop(0, count, finish, 0)
    out_ref[...] = jnp.zeros_like(out_ref)

    def weight(j, carry):
        out_ref[...] += mm(nb[j], grads[j], TN)
        return carry

    lax.fori_loop(0, count, weight, 0)


def root_back(grad_unit, unit_value, factor_row):
    factor = jnp.broadcast_to(factor_row, (HD, TOK_TILE)).T
    inner = jnp.mean(grad_unit * unit_value, -1, keepdims=True)
    return (factor * (grad_unit - unit_value * inner)).astype(jnp.bfloat16)


def vmem():
    return pl.BlockSpec(memory_space=pltpu.VMEM)


def params():
    return pltpu.CompilerParams(vmem_limit_bytes=VMEM_BYTES)


def per_device(
    count, heads, tokens, mod_shift, mod_scale, mod_gate, qkv_weight, out_weight, teacher, slot_tiles
):
    features = tokens.shape[1]
    part = features // count
    quarter = TOK_TILE // heads
    width_tiles = count // (TT * TH)
    me = lax.axis_index("tile")
    my_head = lax.axis_index("head")
    source_table, target_table = ring_tables(count)
    source = jnp.asarray(source_table)[me]
    target = jnp.asarray(target_table)[me]
    onehot = (source[:, None] == jnp.arange(count, dtype=jnp.int32)[None, :]).astype(jnp.int32)
    rel_tiles = jnp.sum(onehot * slot_tiles[None, :], 1)
    allowed = near_tiles(rel_tiles, rel_tiles, width_tiles)

    out_weights = head_gather_doubling(out_weight, heads)

    bf16, f32 = jnp.bfloat16, jnp.float32
    normed, kv, qq = pl.pallas_call(
        project_kernel,
        out_shape=(
            jax.ShapeDtypeStruct((TOK_TILE, features), bf16),
            jax.ShapeDtypeStruct((2 * TOK_TILE, HD), bf16),
            jax.ShapeDtypeStruct((3 * TOK_TILE + STAT_ROWS, HD), bf16),
        ),
        in_specs=[vmem()] * 4,
        out_specs=(vmem(),) * 3,
        compiler_params=params(),
        name="project",
    )(tokens, mod_shift[None, :], mod_scale[None, :], qkv_weight)

    kv_all = ring_gather(kv, count)
    qq_all = ring_gather(qq, count)

    mine = lax.dynamic_slice_in_dim(normed, my_head * quarter, quarter, 0)
    slices = []
    for index, rel in enumerate(rel_offsets(count)):
        piece = lax.dynamic_slice_in_dim(mine, target[index] * part, part, 1)
        if rel:
            piece = lax.ppermute(piece, "tile", shift_perm(count, -rel))
        slices.append(piece)
    slab = jnp.stack(slices, 0)
    slabs = head_gather_doubling(slab, heads)
    normed_part = jnp.zeros((count, heads, quarter, part), bf16)
    for mask in range(heads):
        normed_part = lax.dynamic_update_slice(
            normed_part, slabs[mask][:, None], (0, my_head ^ mask, 0, 0)
        )
    normed_part = normed_part.reshape(count, TOK_TILE, part)

    attended, inverse = pl.pallas_call(
        functools.partial(attend_kernel, count),
        out_shape=(
            jax.ShapeDtypeStruct((TOK_TILE, HD), bf16),
            jax.ShapeDtypeStruct((1, TOK_TILE), f32),
        ),
        in_specs=[pl.BlockSpec(memory_space=pltpu.SMEM)] + [vmem()] * (1 + count),
        out_specs=(vmem(),) * 2,
        scratch_shapes=[
            pltpu.VMEM((count, TOK_TILE, TOK_TILE), f32),
            pltpu.VMEM((1, TOK_TILE), f32),
            pltpu.VMEM((HD, TOK_TILE), f32),
        ],
        compiler_params=params(),
        name="attend",
    )(allowed, qq, *kv_all)

    attended_all = head_gather_direct(attended, heads)

    chunk = 512
    row = pl.BlockSpec((1, chunk), lambda j: (0, j))
    whole_att = pl.BlockSpec((TOK_TILE, HD), lambda j: (0, 0))
    grad_att, out_term = pl.pallas_call(
        functools.partial(branch_kernel, heads),
        grid=(features // chunk,),
        out_shape=(
            jax.ShapeDtypeStruct((TOK_TILE + STAT_ROWS, HD), bf16),
            jax.ShapeDtypeStruct((HD, features), f32),
        ),
        in_specs=[
            pl.BlockSpec((1, TOK_TILE), lambda j: (0, 0)),
            row,
            pl.BlockSpec((TOK_TILE, chunk), lambda j: (0, j)),
        ]
        + [whole_att] * heads
        + [pl.BlockSpec((HD, chunk), lambda j: (0, j))] * heads,
        out_specs=(
            pl.BlockSpec((TOK_TILE + STAT_ROWS, HD), lambda j: (0, 0)),
            pl.BlockSpec((HD, chunk), lambda j: (0, j)),
        ),
        scratch_shapes=[pltpu.VMEM((TOK_TILE, HD), f32)],
        compiler_params=params(),
        name="branch",
    )(inverse, mod_gate[None, :], teacher, *attended_all, *out_weights)

    ga_all = ring_gather(grad_att, count)

    top = jnp.max(jnp.abs(out_term), 0, keepdims=True)
    power = jnp.floor(jnp.log2(jnp.clip(top, 2.0**-100, 2.0**100))) - 10.0
    scaled = jnp.concatenate(
        [out_term * jnp.exp2(-power), jnp.broadcast_to(power, (16, features))], 0
    ).astype(jnp.float16)
    out_grad = lax.dynamic_slice_in_dim(out_term, me * part, part, 1)
    for index, rel in enumerate(rel_offsets(count)):
        if rel:
            piece = lax.dynamic_slice_in_dim(scaled, target[index] * part, part, 1)
            piece = lax.ppermute(piece, "tile", shift_perm(count, -rel)).astype(f32)
            out_grad += piece[:HD] * jnp.exp2(piece[HD : HD + 1])

    hbm = pl.BlockSpec(memory_space=pl.ANY)
    qkv_grad = pl.pallas_call(
        functools.partial(backward_kernel, count),
        out_shape=jax.ShapeDtypeStruct((part, 3 * HD), f32),
        in_specs=[pl.BlockSpec(memory_space=pltpu.SMEM)] + [hbm] * (3 * count + 1),
        out_specs=vmem(),
        scratch_shapes=[
            pltpu.VMEM((count, 2 * TOK_TILE, HD), bf16),
            pltpu.VMEM((count, 3 * TOK_TILE + STAT_ROWS, HD), bf16),
            pltpu.VMEM((count, TOK_TILE + STAT_ROWS, HD), bf16),
            pltpu.VMEM((count, TOK_TILE, part), bf16),
            pltpu.VMEM((HD, TOK_TILE), f32),
            pltpu.VMEM((count, TOK_TILE, HD), f32),
            pltpu.VMEM((count, TOK_TILE, HD), f32),
            pltpu.VMEM((count, TOK_TILE, 3 * HD), bf16),
            pltpu.SemaphoreType.DMA((3 * count + 1,)),
        ],
        compiler_params=params(),
        name="backward",
    )(allowed, *kv_all, *qq_all, *ga_all, normed_part)
    return (qkv_grad, out_grad)


def solution(mesh):
    return jax.shard_map(
        functools.partial(per_device, mesh.shape["tile"], mesh.shape["head"]),
        mesh=mesh,
        in_specs=(
            P("tile", None),
            P(),
            P(),
            P(),
            P(None, "head"),
            P("head", None),
            P("tile", None),
            P(),
        ),
        out_specs=(P("tile", "head"), P("head", "tile")),
        check_vma=False,
    )
```

```python
import functools
import math

import jax
import jax.numpy as jnp
import numpy as np
from jax import lax
from jax.experimental import pallas as pl
from jax.experimental.pallas import tpu as pltpu
from jax.sharding import PartitionSpec as P

HD = 128
TOK_TILE = 384
LANE_ROWS = TOK_TILE // HD
TT = 1
TH = 4


EPS_NORM = 1e-05
EPS_ROOT = 1e-06
LOSS_WEIGHT = 32.0
EXP_SCALE = math.log2(math.e) / math.sqrt(HD)
ATT_SCALE = 1.0 / math.sqrt(HD)
STAT_ROWS = 32
VMEM_BYTES = 56 * 1024 * 1024

NN = (((1,), (0,)), ((), ()))
NT = (((1,), (1,)), ((), ()))
TN = (((0,), (0,)), ((), ()))


def mm(a, b, dims):
    return lax.dot_general(a, b, dims, preferred_element_type=jnp.float32)


def near_tiles(first_tiles, second_tiles, width_tiles):

    def coords(ids):
        return (ids // (TH * width_tiles), ids // width_tiles % TH, ids % width_tiles)

    ta, ha, wa = coords(first_tiles[:, None])
    tb, hb, wb = coords(second_tiles[None, :])
    close = (jnp.abs(ta - tb) <= 1) & (jnp.abs(ha - hb) <= 1) & (jnp.abs(wa - wb) <= 1)
    return close.astype(jnp.int32)


def split3(row):
    hi = row.astype(jnp.bfloat16).astype(jnp.float32)
    rest = row - hi
    mid = rest.astype(jnp.bfloat16).astype(jnp.float32)
    return [hi, mid, rest - mid]


def pack_rows(rows):
    pieces = [part for row in rows for part in split3(row)]
    pieces.append(jnp.zeros((STAT_ROWS - len(pieces), HD), jnp.float32))
    return jnp.concatenate(pieces, 0).astype(jnp.bfloat16)


def unpack_rows(packed, index):
    wide = packed.astype(jnp.float32)
    rows = []
    for chunk in range(LANE_ROWS):
        at = (index * LANE_ROWS + chunk) * 3
        rows.append(wide[at : at + 1] + wide[at + 1 : at + 2] + wide[at + 2 : at + 3])
    return jnp.concatenate(rows, 1)


def lane_chunks(row):
    return [row[:, c * HD : (c + 1) * HD] for c in range(LANE_ROWS)]


def project_kernel(tok_ref, shift_ref, scale_ref, w_ref, normed_ref, kv_ref, q_ref):
    query_rows, key_rows = [], []
    for chunk in range(LANE_ROWS):
        rows = pl.ds(chunk * HD, HD)
        values_in = tok_ref[rows, :].astype(jnp.float32)
        center = values_in - jnp.mean(values_in, -1, keepdims=True)
        spread = jnp.mean(center * center, -1, keepdims=True)
        normed = (
            center * lax.rsqrt(spread + EPS_NORM) * (1.0 + scale_ref[...]) + shift_ref[...]
        ).astype(jnp.bfloat16)
        normed_ref[rows, :] = normed
        projected = mm(normed, w_ref[...], NN)
        query, key, value = (projected[:, c * HD : (c + 1) * HD] for c in range(3))
        rq = lax.rsqrt(jnp.mean(query * query, -1, keepdims=True) + EPS_ROOT)
        rk = lax.rsqrt(jnp.mean(key * key, -1, keepdims=True) + EPS_ROOT)
        query, key = query * rq, key * rk
        query_b, key_b = query.astype(jnp.bfloat16), key.astype(jnp.bfloat16)
        q_ref[rows, :] = query_b
        q_ref[pl.ds(TOK_TILE + chunk * HD, HD), :] = (
            query - query_b.astype(jnp.float32)
        ).astype(jnp.bfloat16)
        q_ref[pl.ds(2 * TOK_TILE + chunk * HD, HD), :] = (
            key - key_b.astype(jnp.float32)
        ).astype(jnp.bfloat16)
        kv_ref[rows, :] = key_b
        kv_ref[pl.ds(TOK_TILE + chunk * HD, HD), :] = value.astype(jnp.bfloat16)
        query_rows.append(jnp.broadcast_to(rq, (HD, HD)).T[0:1])
        key_rows.append(jnp.broadcast_to(rk, (HD, HD)).T[0:1])
    q_ref[pl.ds(3 * TOK_TILE, STAT_ROWS), :] = pack_rows(query_rows + key_rows)


def attend_kernel(count, allowed_ref, q_ref, kv_ref, att_ref, inv_ref, expo, totals, acc):
    query = q_ref[pl.ds(0, TOK_TILE), :]
    totals[...] = jnp.zeros_like(totals)
    acc[...] = jnp.zeros_like(acc)
    for r in range(count):

        @pl.when(allowed_ref[0, r] != 0)
        def _():
            scores = mm(kv_ref[r, pl.ds(0, TOK_TILE), :], query, NT)
            part = jnp.exp2(scores * EXP_SCALE)
            expo[r] = part
            totals[...] += jnp.sum(part, 0, keepdims=True)

    inverse = 1.0 / totals[...]
    inv_ref[...] = inverse
    for r in range(count):

        @pl.when(allowed_ref[0, r] != 0)
        def _():
            probs = (expo[r] * inverse).astype(jnp.bfloat16)
            acc[...] += mm(kv_ref[r, pl.ds(TOK_TILE, TOK_TILE), :], probs, TN)

    att_ref[...] = acc[...].T.astype(jnp.bfloat16)


def branch_kernel(heads, inv_ref, gate_ref, teacher_ref, *refs):
    own_att, own_w, all_att, all_w, ga_ref, out_ref, acc = refs
    step = pl.program_id(0)

    @pl.when(step == 0)
    def _():
        acc[...] = jnp.zeros_like(acc)

    branch = mm(all_att[0], all_w[0], NN)
    for h in range(1, heads):
        branch += mm(all_att[h], all_w[h], NN)
    gate = gate_ref[...]
    residual = LOSS_WEIGHT * (gate * branch - teacher_ref[...].astype(jnp.float32))
    grad = (gate * residual).astype(jnp.bfloat16)
    out_ref[...] = mm(own_att[...], grad, TN)
    acc[...] += mm(grad, own_w[...], NT)

    @pl.when(step == pl.num_programs(0) - 1)
    def _():
        grad_att = acc[...].astype(jnp.bfloat16)
        ga_ref[pl.ds(0, TOK_TILE), :] = grad_att
        product = grad_att.astype(jnp.float32) * own_att[...].astype(jnp.float32)
        delta = jnp.sum(product.T, 0, keepdims=True)
        ga_ref[pl.ds(TOK_TILE, STAT_ROWS), :] = pack_rows(
            lane_chunks(inv_ref[...]) + lane_chunks(delta)
        )


def backward_kernel(count, allowed_ref, kv, qq, ga, nb, out_ref, dq, dk, dv, grads):
    dk[...] = jnp.zeros_like(dk)
    dv[...] = jnp.zeros_like(dv)
    first = pl.ds(0, TOK_TILE)
    second = pl.ds(TOK_TILE, TOK_TILE)
    stats = pl.ds(TOK_TILE, STAT_ROWS)

    def per_query(i, carry):
        query = qq[i, first, :]
        grad = ga[i, first, :]
        packed = ga[i, stats, :]
        inverse, delta = unpack_rows(packed, 0), unpack_rows(packed, 1)
        dq[...] = jnp.zeros_like(dq)

        def per_key(j, carry):
            @pl.when(allowed_ref[i, j] != 0)
            def _():
                key = kv[j, first, :]
                value = kv[j, second, :]
                scores = mm(key, query, NT)
                probs = jnp.exp2(scores * EXP_SCALE) * inverse
                grad_probs = mm(value, grad, NT)
                grad_scores = (probs * (grad_probs - delta)).astype(jnp.bfloat16)
                dv[j] += mm(probs.astype(jnp.bfloat16), grad, NN)
                dk[j] += mm(grad_scores, query, NN)
                dq[...] += mm(key, grad_scores, TN)

            return carry

        lax.fori_loop(0, count, per_key, 0)
        query_unit = query.astype(jnp.float32) + qq[i, second, :].astype(jnp.float32)
        factor = unpack_rows(qq[i, pl.ds(3 * TOK_TILE, STAT_ROWS), :], 0)
        grads[i, :, pl.ds(0, HD)] = root_back(dq[...].T * ATT_SCALE, query_unit, factor)
        return carry

    lax.fori_loop(0, count, per_query, 0)

    def finish(j, carry):
        key_unit = kv[j, first, :].astype(jnp.float32) + qq[
            j, pl.ds(2 * TOK_TILE, TOK_TILE), :
        ].astype(jnp.float32)
        factor = unpack_rows(qq[j, pl.ds(3 * TOK_TILE, STAT_ROWS), :], 1)
        grads[j, :, pl.ds(HD, HD)] = root_back(dk[j] * ATT_SCALE, key_unit, factor)
        grads[j, :, pl.ds(2 * HD, HD)] = dv[j].astype(jnp.bfloat16)
        return carry

    lax.fori_loop(0, count, finish, 0)
    out_ref[...] = jnp.zeros_like(out_ref)

    def weight(j, carry):
        out_ref[...] += mm(nb[j], grads[j], TN)
        return carry

    lax.fori_loop(0, count, weight, 0)


def root_back(grad_unit, unit_value, factor_row):
    factor = jnp.broadcast_to(factor_row, (HD, TOK_TILE)).T
    inner = jnp.mean(grad_unit * unit_value, -1, keepdims=True)
    return (factor * (grad_unit - unit_value * inner)).astype(jnp.bfloat16)


def vmem():
    return pl.BlockSpec(memory_space=pltpu.VMEM)


def params():
    return pltpu.CompilerParams(vmem_limit_bytes=VMEM_BYTES)


def per_device(
    count, heads, tokens, mod_shift, mod_scale, mod_gate, qkv_weight, out_weight, teacher, slot_tiles
):
    features = tokens.shape[1]
    part = features // count
    quarter = TOK_TILE // heads
    width_tiles = count // (TT * TH)
    me = lax.axis_index("tile")
    my_head = lax.axis_index("head")
    allowed = near_tiles(slot_tiles, slot_tiles, width_tiles)
    mine_allowed = lax.dynamic_slice_in_dim(allowed, me, 1, 0)

    out_weights = lax.all_gather(out_weight, "head")

    bf16, f32 = jnp.bfloat16, jnp.float32
    normed, kv, qq = pl.pallas_call(
        project_kernel,
        out_shape=(
            jax.ShapeDtypeStruct((TOK_TILE, features), bf16),
            jax.ShapeDtypeStruct((2 * TOK_TILE, HD), bf16),
            jax.ShapeDtypeStruct((3 * TOK_TILE + STAT_ROWS, HD), bf16),
        ),
        in_specs=[vmem()] * 4,
        out_specs=(vmem(),) * 3,
        compiler_params=params(),
        name="project",
    )(tokens, mod_shift[None, :], mod_scale[None, :], qkv_weight)

    kv_all = lax.all_gather(kv, "tile")
    qq_all = lax.all_gather(qq, "tile")

    mine = lax.dynamic_slice_in_dim(normed, my_head * quarter, quarter, 0)
    mine = mine.reshape(quarter, count, part).transpose(1, 0, 2)
    slab = lax.all_to_all(mine, "tile", 0, 0, tiled=True)
    normed_part = lax.all_gather(slab, "head", axis=1, tiled=True)

    attended, inverse = pl.pallas_call(
        functools.partial(attend_kernel, count),
        out_shape=(
            jax.ShapeDtypeStruct((TOK_TILE, HD), bf16),
            jax.ShapeDtypeStruct((1, TOK_TILE), f32),
        ),
        in_specs=[pl.BlockSpec(memory_space=pltpu.SMEM)] + [vmem()] * 2,
        out_specs=(vmem(),) * 2,
        scratch_shapes=[
            pltpu.VMEM((count, TOK_TILE, TOK_TILE), f32),
            pltpu.VMEM((1, TOK_TILE), f32),
            pltpu.VMEM((HD, TOK_TILE), f32),
        ],
        compiler_params=params(),
        name="attend",
    )(mine_allowed, qq, kv_all)

    attended_all = lax.all_gather(attended, "head")

    chunk = 512
    row = pl.BlockSpec((1, chunk), lambda j: (0, j))
    whole_att = pl.BlockSpec((TOK_TILE, HD), lambda j: (0, 0))
    grad_att, out_term = pl.pallas_call(
        functools.partial(branch_kernel, heads),
        grid=(features // chunk,),
        out_shape=(
            jax.ShapeDtypeStruct((TOK_TILE + STAT_ROWS, HD), bf16),
            jax.ShapeDtypeStruct((HD, features), f32),
        ),
        in_specs=[
            pl.BlockSpec((1, TOK_TILE), lambda j: (0, 0)),
            row,
            pl.BlockSpec((TOK_TILE, chunk), lambda j: (0, j)),
        ]
        + [whole_att, pl.BlockSpec((HD, chunk), lambda j: (0, j))]
        + [
            pl.BlockSpec((heads, TOK_TILE, HD), lambda j: (0, 0, 0)),
            pl.BlockSpec((heads, HD, chunk), lambda j: (0, 0, j)),
        ],
        out_specs=(
            pl.BlockSpec((TOK_TILE + STAT_ROWS, HD), lambda j: (0, 0)),
            pl.BlockSpec((HD, chunk), lambda j: (0, j)),
        ),
        scratch_shapes=[pltpu.VMEM((TOK_TILE, HD), f32)],
        compiler_params=params(),
        name="branch",
    )(inverse, mod_gate[None, :], teacher, attended, out_weight, attended_all, out_weights)

    ga_all = lax.all_gather(grad_att, "tile")

    top = jnp.max(jnp.abs(out_term), 0, keepdims=True)
    power = jnp.floor(jnp.log2(jnp.clip(top, 2.0**-100, 2.0**100))) - 10.0
    scaled = jnp.concatenate(
        [out_term * jnp.exp2(-power), jnp.broadcast_to(power, (16, features))], 0
    ).astype(jnp.float16)
    pieces = scaled.reshape(HD + 16, count, part).transpose(1, 0, 2)
    pieces = lax.all_to_all(pieces, "tile", 0, 0, tiled=True).astype(f32)
    out_grad = jnp.sum(pieces[:, :HD] * jnp.exp2(pieces[:, HD : HD + 1]), 0)

    qkv_grad = pl.pallas_call(
        functools.partial(backward_kernel, count),
        out_shape=jax.ShapeDtypeStruct((part, 3 * HD), f32),
        in_specs=[pl.BlockSpec(memory_space=pltpu.SMEM)] + [vmem()] * 4,
        out_specs=vmem(),
        scratch_shapes=[
            pltpu.VMEM((HD, TOK_TILE), f32),
            pltpu.VMEM((count, TOK_TILE, HD), f32),
            pltpu.VMEM((count, TOK_TILE, HD), f32),
            pltpu.VMEM((count, TOK_TILE, 3 * HD), bf16),
        ],
        compiler_params=params(),
        name="backward",
    )(allowed, kv_all, qq_all, ga_all, normed_part)
    return (qkv_grad, out_grad)


def solution(mesh):
    return jax.shard_map(
        functools.partial(per_device, mesh.shape["tile"], mesh.shape["head"]),
        mesh=mesh,
        in_specs=(
            P("tile", None),
            P(),
            P(),
            P(),
            P(None, "head"),
            P("head", None),
            P("tile", None),
            P(),
        ),
        out_specs=(P("tile", "head"), P("head", "tile")),
        check_vma=False,
    )
```

```python
import functools
import math

import jax
import jax.numpy as jnp
import numpy as np
from jax import lax
from jax.experimental import pallas as pl
from jax.experimental.pallas import tpu as pltpu
from jax.sharding import PartitionSpec as P

HD = 128
TOK_TILE = 384
LANE_ROWS = TOK_TILE // HD
TT = 1
TH = 4


EPS_NORM = 1e-05
EPS_ROOT = 1e-06
LOSS_WEIGHT = 32.0
EXP_SCALE = math.log2(math.e) / math.sqrt(HD)
ATT_SCALE = 1.0 / math.sqrt(HD)
STAT_ROWS = 32
VMEM_BYTES = 56 * 1024 * 1024

NN = (((1,), (0,)), ((), ()))
NT = (((1,), (1,)), ((), ()))
TN = (((0,), (0,)), ((), ()))


def mm(a, b, dims):
    return lax.dot_general(a, b, dims, preferred_element_type=jnp.float32)


def ring_order(count):
    return [*range(0, count, 2), *range(count - 1 - (count % 2), 0, -2)]


def rel_offsets(count):
    offsets = [0]
    for step in range(1, count // 2 + 1):
        offsets.append(-step)
        if len(offsets) < count:
            offsets.append(step)
    return offsets[:count]


def ring_table(count):
    order = ring_order(count)
    pos = [order.index(slot) for slot in range(count)]
    rels = rel_offsets(count)
    return np.array([[order[(pos[s] + rel) % count] for rel in rels] for s in range(count)], np.int32)


def shift_perm(count, offset):
    order = ring_order(count)
    return [(order[p], order[(p + offset) % count]) for p in range(count)]


def ring_gather(block, count):
    up, down = [block], [block]
    for _ in range(count // 2):
        up.append(lax.ppermute(up[-1], "tile", shift_perm(count, 1)))
    for _ in range((count - 1) // 2):
        down.append(lax.ppermute(down[-1], "tile", shift_perm(count, -1)))
    out = []
    for rel in rel_offsets(count):
        out.append(up[-rel] if rel <= 0 else down[rel])
    return out


def xor_perm(count, mask):
    return [(h, h ^ mask) for h in range(count)]


def head_gather_direct(block, count):
    return [block] + [lax.ppermute(block, "head", xor_perm(count, m)) for m in range(1, count)]


def near_tiles(first_tiles, second_tiles, width_tiles):

    def coords(ids):
        return (ids // (TH * width_tiles), ids // width_tiles % TH, ids % width_tiles)

    ta, ha, wa = coords(first_tiles[:, None])
    tb, hb, wb = coords(second_tiles[None, :])
    close = (jnp.abs(ta - tb) <= 1) & (jnp.abs(ha - hb) <= 1) & (jnp.abs(wa - wb) <= 1)
    return close.astype(jnp.int32)


def near_lists(close):
    count = close.shape[0]
    before = jnp.sum(
        close[:, None, :] * (jnp.arange(count)[None, :] < jnp.arange(count)[:, None])[None], 2
    )
    at = (before[:, None, :] == jnp.arange(count)[None, :, None]) & (close[:, None, :] != 0)
    lists = jnp.sum(at * jnp.arange(count, dtype=jnp.int32)[None, None, :], 2)
    return jnp.concatenate([lists, jnp.sum(close, 1, keepdims=True)], 1).astype(jnp.int32)


def split3(row):
    hi = row.astype(jnp.bfloat16).astype(jnp.float32)
    rest = row - hi
    mid = rest.astype(jnp.bfloat16).astype(jnp.float32)
    return [hi, mid, rest - mid]


def pack_rows(rows):
    pieces = [part for row in rows for part in split3(row)]
    pieces.append(jnp.zeros((STAT_ROWS - len(pieces), HD), jnp.float32))
    return jnp.concatenate(pieces, 0).astype(jnp.bfloat16)


def unpack_rows(packed, index):
    wide = packed.astype(jnp.float32)
    rows = []
    for chunk in range(LANE_ROWS):
        at = (index * LANE_ROWS + chunk) * 3
        rows.append(wide[at : at + 1] + wide[at + 1 : at + 2] + wide[at + 2 : at + 3])
    return jnp.concatenate(rows, 1)


def lane_chunks(row):
    return [row[:, c * HD : (c + 1) * HD] for c in range(LANE_ROWS)]


def project_kernel(tok_ref, shift_ref, scale_ref, w_ref, normed_ref, kv_ref, q_ref, lo_ref):
    query_rows, key_rows = [], []
    for chunk in range(LANE_ROWS):
        rows = pl.ds(chunk * HD, HD)
        values_in = tok_ref[rows, :].astype(jnp.float32)
        center = values_in - jnp.mean(values_in, -1, keepdims=True)
        spread = jnp.mean(center * center, -1, keepdims=True)
        normed = (
            center * lax.rsqrt(spread + EPS_NORM) * (1.0 + scale_ref[...]) + shift_ref[...]
        ).astype(jnp.bfloat16)
        normed_ref[rows, :] = normed
        projected = mm(normed, w_ref[...], NN)
        query, key, value = (projected[:, c * HD : (c + 1) * HD] for c in range(3))
        rq = lax.rsqrt(jnp.mean(query * query, -1, keepdims=True) + EPS_ROOT)
        rk = lax.rsqrt(jnp.mean(key * key, -1, keepdims=True) + EPS_ROOT)
        query, key = query * rq, key * rk
        query_b, key_b = query.astype(jnp.bfloat16), key.astype(jnp.bfloat16)
        q_ref[rows, :] = query_b
        lo_ref[rows, :] = (
            query - query_b.astype(jnp.float32)
        ).astype(jnp.bfloat16)
        lo_ref[pl.ds(TOK_TILE + chunk * HD, HD), :] = (
            key - key_b.astype(jnp.float32)
        ).astype(jnp.bfloat16)
        kv_ref[rows, :] = key_b
        kv_ref[pl.ds(TOK_TILE + chunk * HD, HD), :] = value.astype(jnp.bfloat16)
        query_rows.append(jnp.broadcast_to(rq, (HD, HD)).T[0:1])
        key_rows.append(jnp.broadcast_to(rk, (HD, HD)).T[0:1])
    lo_ref[pl.ds(2 * TOK_TILE, STAT_ROWS), :] = pack_rows(query_rows + key_rows)


def attend_kernel(count, allowed_ref, q_ref, *refs):
    kv_refs = refs[:count]
    att_ref, inv_ref, expo, totals, acc = refs[count:]
    query = q_ref[...]
    totals[...] = jnp.zeros_like(totals)
    acc[...] = jnp.zeros_like(acc)
    for r in range(count):

        @pl.when(allowed_ref[0, r] != 0)
        def _():
            scores = mm(kv_refs[r][pl.ds(0, TOK_TILE), :], query, NT)
            part = jnp.exp2(scores * EXP_SCALE)
            expo[r] = part
            totals[...] += jnp.sum(part, 0, keepdims=True)

    inverse = 1.0 / totals[...]
    inv_ref[...] = inverse
    for r in range(count):

        @pl.when(allowed_ref[0, r] != 0)
        def _():
            probs = (expo[r] * inverse).astype(jnp.bfloat16)
            acc[...] += mm(kv_refs[r][pl.ds(TOK_TILE, TOK_TILE), :], probs, TN)

    att_ref[...] = acc[...].T.astype(jnp.bfloat16)


def branch_kernel(heads, q_ref, inv_ref, gate_ref, teacher_ref, *refs):
    att_refs = refs[:heads]
    my_w, all_w, my_head, qd_ref, out_ref, acc = refs[heads:]
    step = pl.program_id(0)

    @pl.when(step == 0)
    def _():
        acc[...] = jnp.zeros_like(acc)

    branch = mm(att_refs[0][...], my_w[...], NN)
    for mask in range(1, heads):
        branch += mm(att_refs[mask][...], all_w[my_head[0] ^ mask], NN)
    gate = gate_ref[...]
    residual = LOSS_WEIGHT * (gate * branch - teacher_ref[...].astype(jnp.float32))
    grad = (gate * residual).astype(jnp.bfloat16)
    out_ref[...] = mm(att_refs[0][...], grad, TN)
    acc[...] += mm(grad, my_w[...], NT)

    @pl.when(step == pl.num_programs(0) - 1)
    def _():
        grad_att = acc[...].astype(jnp.bfloat16)
        qd_ref[pl.ds(0, TOK_TILE), :] = q_ref[...]
        qd_ref[pl.ds(TOK_TILE, TOK_TILE), :] = grad_att
        product = grad_att.astype(jnp.float32) * att_refs[0][...].astype(jnp.float32)
        delta = jnp.sum(product.T, 0, keepdims=True)
        qd_ref[pl.ds(2 * TOK_TILE, STAT_ROWS), :] = pack_rows(
            lane_chunks(inv_ref[...]) + lane_chunks(delta)
        )


FIRST = pl.ds(0, TOK_TILE)
SECOND = pl.ds(TOK_TILE, TOK_TILE)
STATS = pl.ds(2 * TOK_TILE, STAT_ROWS)


def query_tile(row, near_ref, kv, qd_ref, dq, dk, dv):
    query = qd_ref[FIRST, :]
    grad = qd_ref[SECOND, :]
    packed = qd_ref[STATS, :]
    inverse, delta = unpack_rows(packed, 0), unpack_rows(packed, 1)
    count = near_ref.shape[1] - 1
    near = near_ref[row, count]

    def terms(keys):
        scores = [mm(kv[j, FIRST, :], query, NT) for j in keys]
        grad_probs = [mm(kv[j, SECOND, :], grad, NT) for j in keys]
        probs = [jnp.exp2(s * EXP_SCALE) * inverse for s in scores]
        grad_scores = [
            (p * (g - delta)).astype(jnp.bfloat16) for p, g in zip(probs, grad_probs)
        ]
        value_terms = [mm(p.astype(jnp.bfloat16), grad, NN) for p in probs]
        key_terms = [mm(g, query, NN) for g in grad_scores]
        query_terms = [mm(kv[j, FIRST, :], g, TN) for j, g in zip(keys, grad_scores)]
        total = query_terms[0]
        for term in query_terms[1:]:
            total += term
        dq[...] += total
        for j, value_term, key_term in zip(keys, value_terms, key_terms):
            dv[j] += value_term
            dk[j] += key_term

    dq[...] = jnp.zeros(dq.shape, jnp.float32)

    def two(at, carry):
        terms([near_ref[row, 2 * at], near_ref[row, 2 * at + 1]])
        return carry

    lax.fori_loop(0, near // 2, two, 0)

    @pl.when(near % 2 == 1)
    def _():
        terms([near_ref[row, near - 1]])


def start_all(copies):
    for copy in copies:
        copy.start()
    return copies


def wait_all(copies):
    for copy in copies:
        copy.wait()


def chunk_kernel(count, members, chained, near_ref, *refs):
    size = len(members)
    kv_in, qd_in = refs[:count], refs[count : count + size]
    refs = refs[count + size :]
    if chained:
        prev_k, prev_v, dq_ref, dk_ref, dv_ref, kv, sems, before_k, before_v = refs
    else:
        dq_ref, dk_ref, dv_ref, kv, sems = refs
    loads = start_all(
        [pltpu.make_async_copy(kv_in[r], kv.at[r], sems.at[r]) for r in range(count)]
    )
    if chained:
        late = start_all(
            [
                pltpu.make_async_copy(prev_k, before_k, sems.at[count]),
                pltpu.make_async_copy(prev_v, before_v, sems.at[count + 1]),
            ]
        )
    dk_ref[...] = jnp.zeros(dk_ref.shape, jnp.float32)
    dv_ref[...] = jnp.zeros(dv_ref.shape, jnp.float32)
    wait_all(loads)
    for at, row in enumerate(members):
        query_tile(row, near_ref, kv, qd_in[at], dq_ref.at[at], dk_ref, dv_ref)
    if chained:
        wait_all(late)
        dk_ref[...] += before_k[...]
        dv_ref[...] += before_v[...]


def final_kernel(count, members, near_ref, source_ref, *refs):
    size = len(members)
    kv_in, qd_in, refs = refs[:count], refs[count : 2 * count], refs[2 * count :]
    dq_in, refs = refs[: count - size], refs[count - size :]
    prev_k, prev_v, lo_in, nb_in, out_ref, kv, qd, dq, dk, dv, lo, nb, grads, sems = refs
    at = iter(range(4 * count + 4))

    def copy(src, dst):
        return pltpu.make_async_copy(src, dst, sems.at[next(at)])

    loads = start_all(
        [copy(kv_in[r], kv.at[r]) for r in range(count)]
        + [copy(qd_in[r], qd.at[r]) for r in members]
        + [copy(prev_k, dk), copy(prev_v, dv)]
    )
    rest = [r for r in range(count) if r not in members]
    late = start_all(
        [copy(qd_in[r], qd.at[r]) for r in rest]
        + [copy(dq_in[r], dq.at[pl.ds(r, 1)]) for r in rest]
        + [copy(lo_in, lo), copy(nb_in, nb)]
    )
    wait_all(loads)
    for row in members:
        query_tile(row, near_ref, kv, qd.at[row], dq.at[row], dk, dv)
    wait_all(late)

    def finish(r, carry):
        slot = source_ref[r]
        query_unit = qd[r, FIRST, :].astype(jnp.float32) + lo[slot, FIRST, :].astype(jnp.float32)
        key_unit = kv[r, FIRST, :].astype(jnp.float32) + lo[slot, SECOND, :].astype(jnp.float32)
        packed = lo[slot, STATS, :]
        grads[r, :, pl.ds(0, HD)] = root_back(
            dq[r].T * ATT_SCALE, query_unit, unpack_rows(packed, 0)
        )
        grads[r, :, pl.ds(HD, HD)] = root_back(dk[r] * ATT_SCALE, key_unit, unpack_rows(packed, 1))
        grads[r, :, pl.ds(2 * HD, HD)] = dv[r].astype(jnp.bfloat16)
        return carry

    lax.fori_loop(0, count, finish, 0)
    out_ref[...] = jnp.zeros_like(out_ref)

    def weight(r, carry):
        out_ref[...] += mm(nb[source_ref[r]], grads[r], TN)
        return carry

    lax.fori_loop(0, count, weight, 0)


def root_back(grad_unit, unit_value, factor_row):
    factor = jnp.broadcast_to(factor_row, (HD, TOK_TILE)).T
    inner = jnp.mean(grad_unit * unit_value, -1, keepdims=True)
    return (factor * (grad_unit - unit_value * inner)).astype(jnp.bfloat16)


def vmem():
    return pl.BlockSpec(memory_space=pltpu.VMEM)


def params():
    return pltpu.CompilerParams(vmem_limit_bytes=VMEM_BYTES)


def per_device(
    count, heads, tokens, mod_shift, mod_scale, mod_gate, qkv_weight, out_weight, teacher, slot_tiles
):
    features = tokens.shape[1]
    part = features // count
    quarter = TOK_TILE // heads
    width_tiles = count // (TT * TH)
    me = lax.axis_index("tile")
    my_head = lax.axis_index("head")
    source_table = ring_table(count)
    source = jnp.asarray(source_table)[me]
    onehot = (source[:, None] == jnp.arange(count, dtype=jnp.int32)[None, :]).astype(jnp.int32)
    rel_tiles = jnp.sum(onehot * slot_tiles[None, :], 1)
    allowed = near_tiles(rel_tiles, rel_tiles, width_tiles)

    near = near_lists(allowed)

    out_weights = lax.all_gather(out_weight, "head")
    my_weight = out_weight

    bf16, f32 = jnp.bfloat16, jnp.float32
    normed, kv, query, low = pl.pallas_call(
        project_kernel,
        out_shape=(
            jax.ShapeDtypeStruct((TOK_TILE, features), bf16),
            jax.ShapeDtypeStruct((2 * TOK_TILE, HD), bf16),
            jax.ShapeDtypeStruct((TOK_TILE, HD), bf16),
            jax.ShapeDtypeStruct((2 * TOK_TILE + STAT_ROWS, HD), bf16),
        ),
        in_specs=[vmem()] * 4,
        out_specs=(vmem(),) * 4,
        compiler_params=params(),
        name="project",
    )(tokens, mod_shift[None, :], mod_scale[None, :], qkv_weight)

    kv_all = ring_gather(kv, count)
    low, normed, *kv_all = lax.optimization_barrier((low, normed, *kv_all))

    attended, inverse = pl.pallas_call(
        functools.partial(attend_kernel, count),
        out_shape=(
            jax.ShapeDtypeStruct((TOK_TILE, HD), bf16),
            jax.ShapeDtypeStruct((1, TOK_TILE), f32),
        ),
        in_specs=[pl.BlockSpec(memory_space=pltpu.SMEM)] + [vmem()] * (1 + count),
        out_specs=(vmem(),) * 2,
        scratch_shapes=[
            pltpu.VMEM((count, TOK_TILE, TOK_TILE), f32),
            pltpu.VMEM((1, TOK_TILE), f32),
            pltpu.VMEM((HD, TOK_TILE), f32),
        ],
        compiler_params=params(),
        name="attend",
    )(allowed, query, *kv_all)

    normed, attended = lax.optimization_barrier((normed, attended))
    mine = lax.dynamic_slice_in_dim(normed, my_head * quarter, quarter, 0)
    mine = mine.reshape(quarter, count, part).transpose(1, 0, 2)
    slab = lax.all_to_all(mine, "tile", 0, 0, tiled=True)
    normed_part = lax.all_gather(slab, "head", axis=1, tiled=True)
    low_all = lax.all_gather(low, "tile")

    attended_all = head_gather_direct(attended, heads)

    chunk = 512
    row = pl.BlockSpec((1, chunk), lambda j: (0, j))
    whole_att = pl.BlockSpec((TOK_TILE, HD), lambda j: (0, 0))
    qd, out_term = pl.pallas_call(
        functools.partial(branch_kernel, heads),
        grid=(features // chunk,),
        out_shape=(
            jax.ShapeDtypeStruct((2 * TOK_TILE + STAT_ROWS, HD), bf16),
            jax.ShapeDtypeStruct((HD, features), f32),
        ),
        in_specs=[
            whole_att,
            pl.BlockSpec((1, TOK_TILE), lambda j: (0, 0)),
            row,
            pl.BlockSpec((TOK_TILE, chunk), lambda j: (0, j)),
        ]
        + [whole_att] * heads
        + [
            pl.BlockSpec((HD, chunk), lambda j: (0, j)),
            pl.BlockSpec((heads, HD, chunk), lambda j: (0, 0, j)),
            pl.BlockSpec(memory_space=pltpu.SMEM),
        ],
        out_specs=(
            pl.BlockSpec((2 * TOK_TILE + STAT_ROWS, HD), lambda j: (0, 0)),
            pl.BlockSpec((HD, chunk), lambda j: (0, j)),
        ),
        scratch_shapes=[pltpu.VMEM((TOK_TILE, HD), f32)],
        compiler_params=params(),
        name="branch",
    )(
        query,
        inverse,
        mod_gate[None, :],
        teacher,
        *attended_all,
        my_weight,
        out_weights,
        my_head.astype(jnp.int32)[None],
    )

    top = jnp.max(jnp.abs(out_term), 0, keepdims=True)
    power = jnp.floor(jnp.log2(jnp.clip(top, 2.0**-100, 2.0**100))) - 10.0
    scaled = jnp.concatenate(
        [out_term * jnp.exp2(-power), jnp.broadcast_to(power, (16, features))], 0
    ).astype(jnp.float16)
    pieces = scaled.reshape(HD + 16, count, part).transpose(1, 0, 2)
    pieces = lax.all_to_all(pieces, "tile", 0, 0, tiled=True).astype(f32)
    out_grad = jnp.sum(pieces[:, :HD] * jnp.exp2(pieces[:, HD : HD + 1]), 0)

    smem = pl.BlockSpec(memory_space=pltpu.SMEM)
    hbm = pl.BlockSpec(memory_space=pl.ANY)
    sums = jax.ShapeDtypeStruct((count, TOK_TILE, HD), f32)
    sums_vmem = pltpu.VMEM((count, TOK_TILE, HD), f32)
    kv_vmem = pltpu.VMEM((count, 2 * TOK_TILE, HD), bf16)
    qd_all, dq_all, prev = [qd], [], ()
    up, down, step = qd, qd, 0
    while True:
        step += 1
        arrived = list(range(max(0, 2 * step - 3), 2 * step - 1))
        up = lax.ppermute(up, "tile", shift_perm(count, 1))
        if 2 * step < count:
            down = lax.ppermute(down, "tile", shift_perm(count, -1))
        if 2 * step == count:
            break
        dq, *prev = pl.pallas_call(
            functools.partial(chunk_kernel, count, arrived, bool(prev)),
            out_shape=(
                jax.ShapeDtypeStruct((len(arrived), HD, TOK_TILE), f32),
                sums,
                sums,
            ),
            in_specs=[smem] + [hbm] * count + [vmem()] * len(arrived) + [hbm] * len(prev),
            out_specs=(vmem(),) * 3,
            scratch_shapes=[kv_vmem, pltpu.SemaphoreType.DMA((count + 2,))]
            + [sums_vmem] * len(prev),
            compiler_params=params(),
            name=f"backward{step}",
        )(near, *kv_all, *[qd_all[r] for r in arrived], *prev)
        dq_all += [lax.slice_in_dim(dq, k, k + 1) for k in range(len(arrived))]
        qd_all += [up, down]
    qd_all.append(up)
    members = list(range(len(dq_all), count))

    qkv_grad = pl.pallas_call(
        functools.partial(final_kernel, count, members),
        out_shape=jax.ShapeDtypeStruct((part, 3 * HD), f32),
        in_specs=[smem] * 2 + [hbm] * (2 * count + len(dq_all) + 4),
        out_specs=vmem(),
        scratch_shapes=[
            kv_vmem,
            pltpu.VMEM((count, 2 * TOK_TILE + STAT_ROWS, HD), bf16),
            pltpu.VMEM((count, HD, TOK_TILE), f32),
            sums_vmem,
            sums_vmem,
            pltpu.VMEM((count, 2 * TOK_TILE + STAT_ROWS, HD), bf16),
            pltpu.VMEM((count, TOK_TILE, part), bf16),
            pltpu.VMEM((count, TOK_TILE, 3 * HD), bf16),
            pltpu.SemaphoreType.DMA((4 * count + 4,)),
        ],
        compiler_params=params(),
        name="final",
    )(near, source, *kv_all, *qd_all, *dq_all, *prev, low_all, normed_part)
    return (qkv_grad, out_grad)


def solution(mesh):
    return jax.shard_map(
        functools.partial(per_device, mesh.shape["tile"], mesh.shape["head"]),
        mesh=mesh,
        in_specs=(
            P("tile", None),
            P(),
            P(),
            P(),
            P(None, "head"),
            P("head", None),
            P("tile", None),
            P(),
        ),
        out_specs=(P("tile", "head"), P("head", "tile")),
        check_vma=False,
    )
```
